32 devices in a mesh: groups: 2 (over y), row: 4 (over z), col: 4 (over x, core).
Axes of the slice: x: 2, y: 2, z: 4, core: 2. Of those that a mesh axis runs over, the one named last changes fastest.
Arguments:
- activations: bfloat16 [4096, 8192], P('groups', ('row', 'col')), parts along dimension 0, may hold values from -6 to 6
- basis_in: bfloat16 [16384, 512], P(('groups', 'row', 'col')), parts along dimension 0, may hold values from -0.09375 to 0.09375
- gradients: bfloat16 [4096, 28672], P('groups', 'row'), parts along dimension 0, may hold values from -6 to 6
- basis_out: bfloat16 [57344, 1536], P(('groups', 'row'), 'col'), parts along dimension 0, may hold values from -0.03125 to 0.03125
- token_ids: int32 [4, 512], replicated, may hold values from 0 to 31999, as said below
Outputs:
- correction: float32 [1024, 1536], P(('groups', 'row'), 'col'), parts along dimension 0
The draws below stay inside these ranges and needn't reach their ends.
There are 2 independent parts, one for each index of `groups`. The reference program is written for one: setup_inputs(seed, part) draws one part's arguments, and reference() takes and returns one part's arrays. A program takes and returns all parts, laid end to end along the dimension named above; an argument that names none is the same for every part. Nothing has to cross between parts.
Inputs may be any that keep to these rules, and one draw needn't show every extreme that they name: `token_ids`: 0 marks padding and fills only the tail of a sequence; the first sequence has no padding and every sequence has 256 or more tokens that are not padding.
All inputs are finite; a program needn't handle non-finite values.
Results may differ from the reference program's by a relative error of at most 0.0034.
Values may be sent and summed in bfloat16 or wider, within the bound.
No kernel may reach another device: no remote copies, remote signals or barrier semaphores. Data moves between devices by JAX's collectives and lax.ppermute only.
A program may use at most 128 MiB of HBM per device.

```python
import jax
import jax.numpy as jnp
from jax import lax

D_IN = 8192
D_OUT = 28672
VOCAB = 32000
KA = 512
KG = 1536
SEQS = 4
SEQ_LEN = 512
TOKENS = 2048


def draw_token_ids(key, part):
    key = jax.random.fold_in(key, 7)
    key_len, key_ids = jax.random.split(key)
    lengths = jax.random.randint(key_len, (SEQS,), SEQ_LEN // 2, SEQ_LEN + 1)
    lengths = lengths.at[0].set(SEQ_LEN)
    values = jax.random.randint(key_ids, (SEQS, SEQ_LEN), 1, VOCAB)
    positions = jnp.arange(SEQ_LEN, dtype=jnp.int32)[None, :]
    return jnp.where(positions < lengths[:, None], values, 0).astype(jnp.int32)


def with_spikes(entries, own_key, source, target, parts, factor):
    def block_of(axis_at):
        return (jnp.arange(entries.shape[axis_at]) // (entries.shape[axis_at] // parts)).reshape((-1,) + (1,) * (entries.ndim - 1 - axis_at))

    first = jax.random.permutation(own_key, parts)[block_of(target)]
    second = (block_of(target) + parts // 2) % parts
    return jnp.where((block_of(source) == first) | (block_of(source) == second), factor * entries, entries)


def levels(key, dims, shards, least, top_value):
    def one(axis_at, parts):
        heights = jax.random.uniform(jax.random.fold_in(jax.random.fold_in(key, 6), axis_at), (parts,), jnp.float32, least / len(shards), top_value / len(shards))
        return jnp.repeat(jnp.exp(heights), dims[axis_at] // parts).reshape((-1,) + (1,) * (len(dims) - axis_at - 1))

    loudness = one(*shards[0])
    for cut in shards[1:]:
        loudness = loudness * one(*cut)
    return loudness


def centred(stream_key, shape, width, bound, shards=(), kind=jnp.bfloat16):
    values = jax.random.normal(stream_key, shape, jnp.float32) * width
    if len(shards) > 0:
        values = levels(stream_key, shape, shards, -0.22, 0.18) * values
    return jnp.clip(values, min=-bound, max=bound).astype(kind)


def noise_with(rng, shape, deviation, bound, shards, heavy, kind=jnp.bfloat16):
    entries = deviation * jax.random.normal(rng, shape, jnp.float32)
    if shards:
        entries = entries * levels(rng, shape, shards, -0.22, 0.18)
    return jnp.clip(with_spikes(entries, jax.random.fold_in(rng, 3), *heavy), -bound, bound).astype(kind)


def setup_inputs(seed: int = 0, part: int = 0) -> dict:
    seeds = jax.random.split(jax.random.key(seed), 6)
    part_splits = jax.random.split(jax.random.fold_in(seeds[5], part), 6)
    activations = centred(part_splits[0], (TOKENS, D_IN), 1.0, 6.0, ((1, 16),))
    basis_in = noise_with(part_splits[1], (D_IN, KA), D_IN ** -0.5, 0.09375, ((0, 16),), (0, 1, 16, 2.0))
    gradients = centred(part_splits[2], (TOKENS, D_OUT), 1.0, 6.0, ((1, 4),))
    basis_out = centred(part_splits[3], (D_OUT, KG), D_OUT ** -0.5, 0.03125, ((0, 4), (1, 4)))
    token_ids = draw_token_ids(jax.random.fold_in(seeds[5], 71), part)
    return dict(activations=activations, basis_in=basis_in, gradients=gradients, basis_out=basis_out, token_ids=token_ids)


def reference(activations, basis_in, gradients, basis_out, token_ids):
    keep_mask = (token_ids != 0).astype(jnp.float32)
    counts = lax.optimization_barrier(jnp.sum(keep_mask, axis=1))
    scales = 1.0 / jnp.sqrt(counts)
    rot_act = jnp.dot(activations, basis_in, preferred_element_type=jnp.float32).astype(jnp.bfloat16)
    rot_act = rot_act * keep_mask.reshape(-1, 1).astype(jnp.bfloat16)
    rot_grad = jnp.dot(gradients, basis_out, preferred_element_type=jnp.float32).astype(jnp.bfloat16)
    act_blocks = rot_act.astype(jnp.float32).reshape(SEQS, SEQ_LEN, KA)
    grad_blocks = rot_grad.astype(jnp.float32).reshape(SEQS, SEQ_LEN, KG)
    products = jnp.einsum('sla,slc->sac', act_blocks, grad_blocks, precision=lax.Precision.HIGHEST)
    products = products * scales[:, None, None]
    return lax.optimization_barrier(jnp.mean(products * products, axis=0))
```

```python
import functools

import jax
import jax.numpy as jnp
from jax import lax
from jax.experimental import pallas as pl
from jax.experimental.pallas import tpu as pltpu
from jax.sharding import PartitionSpec as P

VMEM = pl.BlockSpec(memory_space=pltpu.VMEM)
SMEM = pl.BlockSpec(memory_space=pltpu.SMEM)
ANY = pl.BlockSpec(memory_space=pl.ANY)
ACT_UP = 4.0
GRAD_UP = 8.0
CUTS = 4


def plain_shards(activations, basis_in, gradients, basis_out, token_ids):
    sequences = token_ids.shape[0]
    keep_mask = (token_ids != 0).astype(jnp.float32)
    counts = jnp.sum(keep_mask, axis=1)
    scales = 1.0 / jnp.sqrt(counts)
    flat_keep = keep_mask.reshape(1, -1).astype(jnp.bfloat16)
    act_share = lax.psum_scatter(
        lax.dot_general(
            basis_in, activations, (((0,), (1,)), ((), ())), preferred_element_type=jnp.float32
        ),
        ("row", "col"),
        scatter_dimension=0,
        tiled=True,
    ).astype(jnp.bfloat16)
    act_local = lax.all_gather(act_share, "col", axis=0, tiled=True) * flat_keep
    partial_value = jnp.dot(gradients, basis_out, preferred_element_type=jnp.float32)
    rot_grad = lax.psum(partial_value, "row").astype(jnp.bfloat16)
    height = act_local.shape[0]
    width = rot_grad.shape[1]
    act_blocks = act_local.reshape(height, sequences, -1)
    grad_blocks = rot_grad.reshape(sequences, -1, width)
    products = jnp.einsum(
        "rsl,slc->rsc", act_blocks, grad_blocks, preferred_element_type=jnp.float32
    )
    products = products * scales[None, :, None]
    return jnp.mean(products * products, axis=1)


def act_kernel(where, act, basis, send_far, send_near, keep_far, keep_near):
    length = send_far.shape[2]
    half = send_far.shape[1]
    z, core = where[0], where[1]
    for mine, far, near in ((False, send_far, send_near), (True, keep_far, keep_near)):
        which = core if mine else 1 - core
        weights = basis[:, pl.ds(pl.multiple_of(which * half, half), half)]
        for slot, step in ((0, 1), (1, 3)):
            rows = act[pl.ds(pl.multiple_of((z ^ step) * length, length), length), :]
            far[slot] = lax.dot_general(
                weights, rows, (((0,), (1,)), ((), ())), preferred_element_type=jnp.float32
            )
        for slot, step in ((0, 0), (1, 2)):
            rows = act[pl.ds(pl.multiple_of((z ^ step) * length, length), length), :]
            near[slot] = lax.dot_general(
                weights, rows, (((0,), (1,)), ((), ())), preferred_element_type=jnp.float32
            )


def rotate_act(where, activations, basis_in, length):
    half = basis_in.shape[1] // 2
    shape = jax.ShapeDtypeStruct((2, half, length), jnp.float32)
    return pl.pallas_call(
        act_kernel,
        in_specs=[SMEM, VMEM, VMEM],
        out_specs=[VMEM] * 4,
        out_shape=[shape] * 4,
        compiler_params=pltpu.CompilerParams(vmem_limit_bytes=24 * 2**20),
    )(where, activations, basis_in)


def grad_kernel(block, gradients, basis, out, buffer, total, sems):
    length, depth = buffer.shape
    cut = depth // CUTS
    start = pl.multiple_of(block[0] * length, length)
    copies = []
    for i in range(CUTS):
        copy = pltpu.make_async_copy(
            gradients.at[pl.ds(start, length), pl.ds(i * cut, cut)],
            buffer.at[:, pl.ds(i * cut, cut)],
            sems.at[i],
        )
        copy.start()
        copies.append(copy)
    for i in range(CUTS):
        copies[i].wait()
        part = lax.dot_general(
            basis[i * cut : (i + 1) * cut, :],
            buffer[:, i * cut : (i + 1) * cut],
            (((0,), (1,)), ((), ())),
            preferred_element_type=jnp.float32,
        )
        if i == 0:
            total[...] = part
        elif i < CUTS - 1:
            total[...] += part
        else:
            out[...] = total[...] + part


def rotate_grad(block, gradients, basis_out, length):
    depth, width = basis_out.shape
    return pl.pallas_call(
        grad_kernel,
        in_specs=[SMEM, ANY, VMEM],
        out_specs=VMEM,
        out_shape=jax.ShapeDtypeStruct((width, length), jnp.float32),
        scratch_shapes=[
            pltpu.VMEM((length, depth), jnp.bfloat16),
            pltpu.VMEM((width, length), jnp.float32),
            pltpu.SemaphoreType.DMA((CUTS,)),
        ],
        compiler_params=pltpu.CompilerParams(vmem_limit_bytes=24 * 2**20),
        cost_estimate=pl.CostEstimate(
            flops=2 * length * depth * width, bytes_accessed=2 * length * depth, transcendentals=0
        ),
    )(jnp.reshape(block, (1,)), gradients, basis_out)


def tile_kernel(share, order, scale, act, grad, own, *sends):
    weight = scale[0]
    rows = own.shape[0]
    for slot, out in enumerate((own, *sends)):
        piece = act[pl.ds(pl.multiple_of(order[slot] * rows, rows), rows), :]
        product = lax.dot_general(
            piece, grad[...], (((1,), (1,)), ((), ())), preferred_element_type=jnp.float32
        )
        product = product * weight
        out[...] = (product * product * share).astype(out.dtype)


def make_tile(order, scale, act, grad, sequences):
    rows, width = act.shape[0] // sequences, grad.shape[0]
    return pl.pallas_call(
        functools.partial(tile_kernel, 1.0 / sequences),
        in_specs=[SMEM, SMEM, VMEM, VMEM],
        out_specs=[VMEM] * sequences,
        out_shape=[jax.ShapeDtypeStruct((rows, width), jnp.float32)]
        + [jax.ShapeDtypeStruct((rows, width), jnp.bfloat16)] * (sequences - 1),
        compiler_params=pltpu.CompilerParams(vmem_limit_bytes=16 * 2**20),
    )(order, scale, act, grad)


def swap(value, axis, step, size=4):
    return lax.ppermute(value, axis, [(i, i ^ step) for i in range(size)])


def pack(value, up):
    return (value * up).astype(jnp.float16)


def unpack(value, up):
    return value.astype(jnp.float32) * (1.0 / up)


def line_shards(activations, basis_in, gradients, basis_out, token_ids):
    sequences, length = token_ids.shape
    z = lax.axis_index("row").astype(jnp.int32)
    place = lax.axis_index("col").astype(jnp.int32)
    core, x = place & 1, place >> 1
    quarter = basis_in.shape[1] // 4

    send_far, send_near, keep_far, keep_near = rotate_act(
        jnp.stack([z, core]), activations, basis_in, length
    )
    far = keep_far + unpack(swap(pack(send_far, ACT_UP), "col", 1), ACT_UP)
    near = keep_near + unpack(swap(pack(send_near, ACT_UP), "col", 1), ACT_UP)

    def over_x(value):
        mine = lax.dynamic_slice_in_dim(value, x * quarter, quarter, 1)
        other = lax.dynamic_slice_in_dim(value, (1 - x) * quarter, quarter, 1)
        return mine + unpack(swap(pack(other, ACT_UP), "col", 2), ACT_UP)

    far, near = over_x(far), over_x(near)

    third = rotate_grad(z ^ 3, gradients, basis_out, length)
    got_third = unpack(swap(pack(third, GRAD_UP), "row", 1), GRAD_UP)
    second = rotate_grad(z ^ 2, gradients, basis_out, length)
    first = rotate_grad(z ^ 1, gradients, basis_out, length)
    got_first = unpack(swap(pack(first, GRAD_UP), "row", 1), GRAD_UP)
    got_second = unpack(swap(pack(second + got_third, GRAD_UP), "row", 2), GRAD_UP)
    own = rotate_grad(z, gradients, basis_out, length)

    near = near + unpack(swap(pack(far, ACT_UP), "row", 1), ACT_UP)
    act = near[0] + unpack(swap(pack(near[1], ACT_UP), "row", 2), ACT_UP)
    keep_mask = (lax.dynamic_slice_in_dim(token_ids, z, 1, 0) != 0).astype(jnp.float32)
    scale = 1.0 / jnp.sqrt(jnp.sum(keep_mask, axis=1))
    act = act.astype(jnp.bfloat16) * keep_mask.astype(jnp.bfloat16)
    across = swap(act, "col", 2)
    pair = jnp.where(x == 0, jnp.stack([act, across]), jnp.stack([across, act]))
    pair = pair.reshape(2 * quarter, length)
    other = swap(pair, "col", 1)
    whole = jnp.where(core == 0, jnp.stack([pair, other]), jnp.stack([other, pair]))
    whole = whole.reshape(4 * quarter, length)

    grad = (own + got_first + got_second).astype(jnp.bfloat16)
    order = jnp.stack([z, z ^ 3, z ^ 2, z ^ 1])
    tile, to_3, to_2, to_1 = make_tile(order, scale, whole, grad, sequences)
    from_3, from_2, from_1 = swap(to_3, "row", 3), swap(to_2, "row", 2), swap(to_1, "row", 1)
    return (
        tile
        + from_3.astype(jnp.float32)
        + from_2.astype(jnp.float32)
        + from_1.astype(jnp.float32)
    )


def solution(mesh):
    in_specs = (
        P("groups", ("row", "col")),
        P(("groups", "row", "col"), None),
        P("groups", "row"),
        P(("groups", "row"), "col"),
        P(),
    )
    out_specs = P(("groups", "row"), "col")
    rows, columns = mesh.shape["row"], mesh.shape["col"]

    def shards(*arrays):
        fits = rows == 4 and columns == 4 and arrays[4].shape[0] == rows
        return (line_shards if fits else plain_shards)(*arrays)

    return jax.shard_map(shards, mesh=mesh, in_specs=in_specs, out_specs=out_specs, check_vma=False)
```

```python
import jax
import jax.numpy as jnp
from jax import lax
from jax.experimental import pallas as pl
from jax.experimental.pallas import tpu as pltpu
from jax.sharding import PartitionSpec as P

VMEM = pl.BlockSpec(memory_space=pltpu.VMEM)
SMEM = pl.BlockSpec(memory_space=pltpu.SMEM)
HBM = pl.BlockSpec(memory_space=pltpu.HBM)
ACT_UP = 4.0
GRAD_UP = 8.0
CUT = 1024


def plain_shards(activations, basis_in, gradients, basis_out, token_ids):
    sequences = token_ids.shape[0]
    keep_mask = (token_ids != 0).astype(jnp.float32)
    counts = jnp.sum(keep_mask, axis=1)
    scales = 1.0 / jnp.sqrt(counts)
    flat_keep = keep_mask.reshape(1, -1).astype(jnp.bfloat16)
    act_share = lax.psum_scatter(
        lax.dot_general(
            basis_in, activations, (((0,), (1,)), ((), ())), preferred_element_type=jnp.float32
        ),
        ("row", "col"),
        scatter_dimension=0,
        tiled=True,
    ).astype(jnp.bfloat16)
    act_local = lax.all_gather(act_share, "col", axis=0, tiled=True) * flat_keep
    partial_value = jnp.dot(gradients, basis_out, preferred_element_type=jnp.float32)
    rot_grad = lax.psum(partial_value, "row").astype(jnp.bfloat16)
    height = act_local.shape[0]
    width = rot_grad.shape[1]
    act_blocks = act_local.reshape(height, sequences, -1)
    grad_blocks = rot_grad.reshape(sequences, -1, width)
    products = jnp.einsum(
        "rsl,slc->rsc", act_blocks, grad_blocks, preferred_element_type=jnp.float32
    )
    products = products * scales[None, :, None]
    return jnp.mean(products * products, axis=1)


def in_hbm(value):
    return pltpu.with_memory_space_constraint(value, pltpu.HBM)


def columns_by_rows(weights, rows):
    return lax.dot_general(
        weights, rows, (((0,), (1,)), ((), ())), preferred_element_type=jnp.float32
    )


def pieces(depth):
    return [(at, min(CUT, depth - at)) for at in range(0, depth, CUT)]


def fetch_block(block, gradients, buffer, sems):
    length, depth = buffer.shape
    start = pl.multiple_of(block * length, length)
    return [
        pltpu.make_async_copy(
            gradients.at[pl.ds(start, length), pl.ds(at, size)],
            buffer.at[:, pl.ds(at, size)],
            sems.at[i],
        )
        for i, (at, size) in enumerate(pieces(depth))
    ]


def rotate_block(copies, weights, buffer, total, out):
    edges = pieces(buffer.shape[1])
    for i, (at, size) in enumerate(edges):
        for copy in copies[i]:
            copy.wait()
        part = columns_by_rows(weights[at : at + size, :], buffer[:, at : at + size])
        if i == 0:
            total[...] = part
        elif i < len(edges) - 1:
            total[...] += part
        else:
            out[...] = total[...] + part


def first_kernel(block, gradients, basis, out, weights, buffer, total, grad_sems, basis_sems):
    copies = []
    edges = pieces(buffer.shape[1])
    for i, copy in enumerate(fetch_block(block[0], gradients, buffer, grad_sems)):
        at, size = edges[i]
        part = pltpu.make_async_copy(
            basis.at[pl.ds(at, size), :], weights.at[pl.ds(at, size), :], basis_sems.at[i]
        )
        part.start()
        copy.start()
        copies.append((part, copy))
    rotate_block(copies, weights, buffer, total, out)


def rotate_first(block, gradients, basis_out, length):
    depth, width = basis_out.shape
    steps = len(pieces(depth))
    return pl.pallas_call(
        first_kernel,
        in_specs=[SMEM, HBM, HBM],
        out_specs=VMEM,
        out_shape=jax.ShapeDtypeStruct((width, length), jnp.float32),
        scratch_shapes=[
            pltpu.VMEM((depth, width), basis_out.dtype),
            pltpu.VMEM((length, depth), jnp.bfloat16),
            pltpu.VMEM((width, length), jnp.float32),
            pltpu.SemaphoreType.DMA((steps,)),
            pltpu.SemaphoreType.DMA((steps,)),
        ],
        compiler_params=pltpu.CompilerParams(vmem_limit_bytes=18 * 2**20),
        cost_estimate=pl.CostEstimate(
            flops=2 * length * depth * width,
            bytes_accessed=2 * depth * (length + width),
            transcendentals=0,
        ),
    )(jnp.reshape(block, (1,)), in_hbm(gradients), in_hbm(basis_out))


def grad_kernel(block, gradients, basis, out, buffer, total, sems):
    copies = fetch_block(block[0], gradients, buffer, sems)
    for copy in copies:
        copy.start()
    rotate_block([(copy,) for copy in copies], basis, buffer, total, out)


def rotate_grad(block, gradients, basis, length):
    depth, width = basis.shape
    return pl.pallas_call(
        grad_kernel,
        in_specs=[SMEM, HBM, VMEM],
        out_specs=VMEM,
        out_shape=jax.ShapeDtypeStruct((width, length), jnp.float32),
        scratch_shapes=[
            pltpu.VMEM((length, depth), jnp.bfloat16),
            pltpu.VMEM((width, length), jnp.float32),
            pltpu.SemaphoreType.DMA((len(pieces(depth)),)),
        ],
        compiler_params=pltpu.CompilerParams(vmem_limit_bytes=12 * 2**20),
        cost_estimate=pl.CostEstimate(flops=1, bytes_accessed=1, transcendentals=0),
    )(jnp.reshape(block, (1,)), in_hbm(gradients), pltpu.with_memory_space_constraint(basis, pltpu.VMEM))


def act_kernel(where, act, basis, far_act, far_basis, *outs):
    quarter, length = outs[0].shape
    z, core, x = where[0], where[1], where[2]
    span = pl.ds(pl.multiple_of(core * 2 * quarter, 2 * quarter), 2 * quarter)
    near = basis[:, span]
    far = far_basis[:, span]
    for i, step in enumerate((3, 2, 1, 0)):
        rows = pl.ds(pl.multiple_of((z ^ step) * length, length), length)
        product = columns_by_rows(near, act[rows, :]) + columns_by_rows(far, far_act[rows, :])
        low, high = product[:quarter], product[quarter:]
        outs[2 * i][...] = jnp.where(x == 0, low, high)
        outs[2 * i + 1][...] = jnp.where(x == 0, high, low)


def rotate_act(where, activations, basis_in, far_act, far_basis, length):
    shape = jax.ShapeDtypeStruct((basis_in.shape[1] // 4, length), jnp.float32)
    return pl.pallas_call(
        act_kernel,
        in_specs=[SMEM, VMEM, VMEM, VMEM, VMEM],
        out_specs=[VMEM] * 8,
        out_shape=[shape] * 8,
        compiler_params=pltpu.CompilerParams(vmem_limit_bytes=12 * 2**20),
        cost_estimate=pl.CostEstimate(
            flops=2 * activations.size * basis_in.shape[1],
            bytes_accessed=4 * activations.size,
            transcendentals=0,
        ),
    )(where, activations, basis_in, far_act, far_basis)


def tile_kernel(order, ids, act, grad, own, *sends):
    sequences, rows = ids.shape[0], own.shape[0]
    keep = (ids[pl.ds(order[0], 1), :] != 0).astype(jnp.float32)
    weight = 1.0 / jnp.sqrt(jnp.sum(keep, axis=1, keepdims=True))
    keep = keep.astype(jnp.bfloat16)
    for slot, out in enumerate((own, *sends)):
        piece = act[pl.ds(pl.multiple_of(order[slot] * rows, rows), rows), :] * keep
        product = lax.dot_general(
            piece, grad[...], (((1,), (1,)), ((), ())), preferred_element_type=jnp.float32
        )
        product = product * weight
        out[...] = (product * product * (1.0 / sequences)).astype(out.dtype)


def make_tile(order, token_ids, act, grad):
    sequences = token_ids.shape[0]
    rows, width = act.shape[0] // sequences, grad.shape[0]
    return pl.pallas_call(
        tile_kernel,
        in_specs=[SMEM, VMEM, VMEM, VMEM],
        out_specs=[VMEM] * sequences,
        out_shape=[jax.ShapeDtypeStruct((rows, width), jnp.float32)]
        + [jax.ShapeDtypeStruct((rows, width), jnp.bfloat16)] * (sequences - 1),
        compiler_params=pltpu.CompilerParams(vmem_limit_bytes=16 * 2**20),
    )(order, token_ids, act, grad)


def swap(value, axis, step, size=4):
    return lax.ppermute(value, axis, [(i, i ^ step) for i in range(size)])


def pack(value, up):
    return (value * up).astype(jnp.float16)


def unpack(value, up):
    return value.astype(jnp.float32) * (1.0 / up)


def line_shards(activations, basis_in, gradients, basis_out, token_ids):
    length = token_ids.shape[1]
    z = lax.axis_index("row").astype(jnp.int32)
    place = lax.axis_index("col").astype(jnp.int32)
    core, x = place & 1, place >> 1
    quarter = basis_in.shape[1] // 4
    middle = basis_out.shape[1] // 3 * 2
    tie = lax.optimization_barrier
    order = jnp.stack([z, z ^ 3, z ^ 2, z ^ 1])
    where = jnp.stack([z, core, x])

    far_act, far_basis = swap(activations, "col", 1), swap(basis_in, "col", 1)
    third = rotate_first(z ^ 3, gradients, basis_out, length)
    third = pack(third, GRAD_UP)
    got_third = swap(third, "row", 1)

    far_act, far_basis, third, order = tie((far_act, far_basis, third, order))
    mine_3, other_3, mine_2, other_2, mine_1, other_1, mine_0, other_0 = rotate_act(
        where, activations, basis_in, far_act, far_basis, length
    )
    other_a = pack(jnp.stack([other_3, other_2]), ACT_UP)
    other_b = pack(jnp.stack([other_1, other_0]), ACT_UP)
    got_a, got_b = swap(other_a, "col", 2), swap(other_b, "col", 2)

    block, other_a, other_b = tie((z ^ 2, other_a, other_b))
    second = rotate_first(block, gradients, basis_out, length)
    got_third, second = tie((got_third, second))
    second = second + unpack(got_third, GRAD_UP)
    upper_2, lower_2 = pack(second[:middle], GRAD_UP), pack(second[middle:], GRAD_UP)
    got_upper_2 = swap(upper_2, "row", 2)
    got_a, upper_2 = tie((got_a, upper_2))
    got_a = unpack(got_a, ACT_UP)
    act_3 = pack(mine_3 + got_a[0], ACT_UP)
    over_3 = swap(act_3, "row", 1)

    block, act_3, upper_2 = tie((z ^ 1, act_3, upper_2))
    first = rotate_grad(block, gradients, basis_out, length)
    first_out = pack(first, GRAD_UP)
    got_b, over_3, first_out = tie((got_b, over_3, first_out))
    got_b = unpack(got_b, ACT_UP)
    act_2 = mine_2 + got_a[1] + unpack(over_3, ACT_UP)
    act_2 = pack(act_2, ACT_UP)
    over_2 = swap(act_2, "row", 2)
    act_1 = pack(mine_1 + got_b[0], ACT_UP)
    over_1 = swap(act_1, "row", 1)
    act_0 = mine_0 + got_b[1]
    lower_2, act_2, act_0 = tie((lower_2, act_2, act_0))
    got_lower_2 = swap(lower_2, "row", 2)
    got_first = swap(first_out, "row", 1)

    block, act_2, act_1, lower_2, first_out = tie((z, act_2, act_1, lower_2, first_out))
    own = rotate_grad(block, gradients, basis_out, length)
    over_1, over_2, got_upper_2, own = tie((over_1, over_2, got_upper_2, own))
    act = act_0 + unpack(over_1, ACT_UP) + unpack(over_2, ACT_UP)
    act = act.astype(jnp.bfloat16)
    across = swap(act, "col", 2)
    pair = jnp.where(x == 0, jnp.stack([act, across]), jnp.stack([across, act]))
    pair = pair.reshape(2 * quarter, length)
    other = swap(pair, "col", 1)
    whole = jnp.where(core == 0, jnp.stack([pair, other]), jnp.stack([other, pair]))
    whole = whole.reshape(4 * quarter, length)

    got_second = jnp.concatenate([got_upper_2, got_lower_2])
    grad = own + unpack(got_first, GRAD_UP) + unpack(got_second, GRAD_UP)
    tile, to_3, to_2, to_1 = make_tile(order, token_ids, whole, grad.astype(jnp.bfloat16))
    from_3, from_2, from_1 = swap(to_3, "row", 3), swap(to_2, "row", 2), swap(to_1, "row", 1)
    return (
        tile
        + from_3.astype(jnp.float32)
        + from_2.astype(jnp.float32)
        + from_1.astype(jnp.float32)
    )


def solution(mesh):
    in_specs = (
        P("groups", ("row", "col")),
        P(("groups", "row", "col"), None),
        P("groups", "row"),
        P(("groups", "row"), "col"),
        P(),
    )
    out_specs = P(("groups", "row"), "col")
    rows, columns = mesh.shape["row"], mesh.shape["col"]

    def shards(*arrays):
        fits = rows == 4 and columns == 4 and arrays[4].shape[0] == rows
        return (line_shards if fits else plain_shards)(*arrays)

    return jax.shard_map(shards, mesh=mesh, in_specs=in_specs, out_specs=out_specs, check_vma=False)
```

```python
import jax
import jax.numpy as jnp
from jax import lax
from jax.experimental import pallas as pl
from jax.experimental.pallas import tpu as pltpu
from jax.sharding import PartitionSpec as P

VMEM = pl.BlockSpec(memory_space=pltpu.VMEM)
SMEM = pl.BlockSpec(memory_space=pltpu.SMEM)
HBM = pl.BlockSpec(memory_space=pltpu.HBM)
ACT_UP = 4.0
GRAD_UP = 8.0
CUT = 1024


def plain_shards(activations, basis_in, gradients, basis_out, token_ids):
    sequences = token_ids.shape[0]
    keep_mask = (token_ids != 0).astype(jnp.float32)
    counts = jnp.sum(keep_mask, axis=1)
    scales = 1.0 / jnp.sqrt(counts)
    flat_keep = keep_mask.reshape(1, -1).astype(jnp.bfloat16)
    act_share = lax.psum_scatter(
        lax.dot_general(
            basis_in, activations, (((0,), (1,)), ((), ())), preferred_element_type=jnp.float32
        ),
        ("row", "col"),
        scatter_dimension=0,
        tiled=True,
    ).astype(jnp.bfloat16)
    act_local = lax.all_gather(act_share, "col", axis=0, tiled=True) * flat_keep
    partial_value = jnp.dot(gradients, basis_out, preferred_element_type=jnp.float32)
    rot_grad = lax.psum(partial_value, "row").astype(jnp.bfloat16)
    height = act_local.shape[0]
    width = rot_grad.shape[1]
    act_blocks = act_local.reshape(height, sequences, -1)
    grad_blocks = rot_grad.reshape(sequences, -1, width)
    products = jnp.einsum(
        "rsl,slc->rsc", act_blocks, grad_blocks, preferred_element_type=jnp.float32
    )
    products = products * scales[None, :, None]
    return jnp.mean(products * products, axis=1)


def in_hbm(value):
    return pltpu.with_memory_space_constraint(value, pltpu.HBM)


def columns_by_rows(weights, rows):
    return lax.dot_general(
        weights, rows, (((0,), (1,)), ((), ())), preferred_element_type=jnp.float32
    )


def pieces(depth):
    return [(at, min(CUT, depth - at)) for at in range(0, depth, CUT)]


def fetch_block(block, gradients, buffer, sems):
    length, depth = buffer.shape
    start = pl.multiple_of(block * length, length)
    return [
        pltpu.make_async_copy(
            gradients.at[pl.ds(start, length), pl.ds(at, size)],
            buffer.at[:, pl.ds(at, size)],
            sems.at[i],
        )
        for i, (at, size) in enumerate(pieces(depth))
    ]


def rotate_block(copies, weights, buffer, out):
    edges = pieces(buffer.shape[1])
    for i, (at, size) in enumerate(edges):
        for copy in copies[i]:
            copy.wait()
        part = columns_by_rows(weights[at : at + size, :], buffer[:, at : at + size])
        if i == 0:
            out[...] = part
        else:
            out[...] += part


def grad_kernel(block, gradients, basis, out, weights, buffer, grad_sems, basis_sems):
    copies = []
    edges = pieces(buffer.shape[1])
    for i, copy in enumerate(fetch_block(block[0], gradients, buffer, grad_sems)):
        at, size = edges[i]
        part = pltpu.make_async_copy(
            basis.at[pl.ds(at, size), :], weights.at[pl.ds(at, size), :], basis_sems.at[i]
        )
        part.start()
        copy.start()
        copies.append((part, copy))
    rotate_block(copies, weights, buffer, out)


def rotate_grad(block, gradients, basis_out, length):
    depth, width = basis_out.shape
    steps = len(pieces(depth))
    return pl.pallas_call(
        grad_kernel,
        in_specs=[SMEM, HBM, HBM],
        out_specs=VMEM,
        out_shape=jax.ShapeDtypeStruct((width, length), jnp.float32),
        scratch_shapes=[
            pltpu.VMEM((depth, width), basis_out.dtype),
            pltpu.VMEM((length, depth), jnp.bfloat16),
            pltpu.SemaphoreType.DMA((steps,)),
            pltpu.SemaphoreType.DMA((steps,)),
        ],
        compiler_params=pltpu.CompilerParams(vmem_limit_bytes=14 * 2**20),
        cost_estimate=pl.CostEstimate(
            flops=2 * length * depth * width,
            bytes_accessed=2 * depth * (length + width),
            transcendentals=0,
        ),
    )(jnp.reshape(block, (1,)), in_hbm(gradients), in_hbm(basis_out))


def act_kernel(where, act, basis, far_act, far_basis, *outs):
    quarter, length = outs[0].shape
    z, core, x = where[0], where[1], where[2]
    span = pl.ds(pl.multiple_of(core * 2 * quarter, 2 * quarter), 2 * quarter)
    near = basis[:, span]
    far = far_basis[:, span]
    for i, step in enumerate((3, 2, 1, 0)):
        rows = pl.ds(pl.multiple_of((z ^ step) * length, length), length)
        product = columns_by_rows(near, act[rows, :]) + columns_by_rows(far, far_act[rows, :])
        low, high = product[:quarter], product[quarter:]
        outs[2 * i][...] = jnp.where(x == 0, low, high)
        outs[2 * i + 1][...] = jnp.where(x == 0, high, low)


def rotate_act(where, activations, basis_in, far_act, far_basis, length):
    shape = jax.ShapeDtypeStruct((basis_in.shape[1] // 4, length), jnp.float32)
    return pl.pallas_call(
        act_kernel,
        in_specs=[SMEM, VMEM, VMEM, VMEM, VMEM],
        out_specs=[VMEM] * 8,
        out_shape=[shape] * 8,
        compiler_params=pltpu.CompilerParams(vmem_limit_bytes=6 * 2**20),
        cost_estimate=pl.CostEstimate(
            flops=2 * activations.size * basis_in.shape[1],
            bytes_accessed=4 * activations.size,
            transcendentals=0,
        ),
    )(where, activations, basis_in, far_act, far_basis)


def tile_kernel(order, ids, act, grad, own, *sends):
    sequences, rows = ids.shape[0], own.shape[0]
    keep = (ids[pl.ds(order[0], 1), :] != 0).astype(jnp.float32)
    weight = 1.0 / jnp.sqrt(jnp.sum(keep, axis=1, keepdims=True))
    keep = keep.astype(jnp.bfloat16)
    for slot, out in enumerate((own, *sends)):
        piece = act[pl.ds(pl.multiple_of(order[slot] * rows, rows), rows), :] * keep
        product = lax.dot_general(
            piece, grad[...], (((1,), (1,)), ((), ())), preferred_element_type=jnp.float32
        )
        product = product * weight
        out[...] = (product * product * (1.0 / sequences)).astype(out.dtype)


def make_tile(order, token_ids, act, grad):
    sequences = token_ids.shape[0]
    rows, width = act.shape[0] // sequences, grad.shape[0]
    return pl.pallas_call(
        tile_kernel,
        in_specs=[SMEM, VMEM, VMEM, VMEM],
        out_specs=[VMEM] * sequences,
        out_shape=[jax.ShapeDtypeStruct((rows, width), jnp.float32)]
        + [jax.ShapeDtypeStruct((rows, width), jnp.bfloat16)] * (sequences - 1),
        compiler_params=pltpu.CompilerParams(vmem_limit_bytes=16 * 2**20),
        cost_estimate=pl.CostEstimate(flops=1, bytes_accessed=1, transcendentals=0),
    )(order, token_ids, act, grad)


def swap(value, axis, step, size=4):
    return lax.ppermute(value, axis, [(i, i ^ step) for i in range(size)])


def pack(value, up):
    return (value * up).astype(jnp.float16)


def unpack(value, up):
    return value.astype(jnp.float32) * (1.0 / up)


def line_shards(activations, basis_in, gradients, basis_out, token_ids):
    length = token_ids.shape[1]
    z = lax.axis_index("row").astype(jnp.int32)
    place = lax.axis_index("col").astype(jnp.int32)
    core, x = place & 1, place >> 1
    quarter = basis_in.shape[1] // 4
    middle = basis_out.shape[1] // 2
    tie = lax.optimization_barrier
    order = jnp.stack([z, z ^ 3, z ^ 2, z ^ 1])
    where = jnp.stack([z, core, x])

    far_act, far_basis = swap(activations, "col", 1), swap(basis_in, "col", 1)
    third = rotate_grad(z ^ 3, gradients, basis_out, length)
    third = pack(third, GRAD_UP)
    got_third = swap(third, "row", 1)

    far_act, far_basis, third, order = tie((far_act, far_basis, third, order))
    mine_3, other_3, mine_2, other_2, mine_1, other_1, mine_0, other_0 = rotate_act(
        where, activations, basis_in, far_act, far_basis, length
    )
    out_3 = pack(other_3, ACT_UP)
    out_210 = pack(jnp.stack([other_2, other_1, other_0]), ACT_UP)
    got_3 = swap(out_3, "col", 2)
    got_210 = swap(out_210, "col", 2)

    block, out_3, out_210 = tie((z ^ 2, out_3, out_210))
    second = rotate_grad(block, gradients, basis_out, length)
    got_third, second = tie((got_third, second))
    second = second + unpack(got_third, GRAD_UP)
    upper_2, lower_2 = pack(second[:middle], GRAD_UP), pack(second[middle:], GRAD_UP)
    got_upper_2 = swap(upper_2, "row", 2)
    got_3, upper_2 = tie((got_3, upper_2))
    act_3 = pack(mine_3 + unpack(got_3, ACT_UP), ACT_UP)
    over_3 = swap(act_3, "row", 1)

    block, act_3, upper_2 = tie((z ^ 1, act_3, upper_2))
    first = rotate_grad(block, gradients, basis_out, length)
    got_210, over_3, first = tie((got_210, over_3, first))
    act_2 = pack(mine_2 + unpack(got_210[0], ACT_UP) + unpack(over_3, ACT_UP), ACT_UP)
    over_2 = swap(act_2, "row", 2)
    act_1 = pack(mine_1 + unpack(got_210[1], ACT_UP), ACT_UP)
    act_0 = mine_0 + unpack(got_210[2], ACT_UP)
    over_1 = swap(act_1, "row", 1)
    first, act_2, act_1, act_0 = tie((first, act_2, act_1, act_0))
    first_out = pack(first, GRAD_UP)
    got_first = swap(first_out, "row", 1)
    block, first_out = tie((z, first_out))
    own = rotate_grad(block, gradients, basis_out, length)
    over_1, over_2, got_upper_2, own = tie((over_1, over_2, got_upper_2, own))
    act = act_0 + unpack(over_1, ACT_UP) + unpack(over_2, ACT_UP)
    act = act.astype(jnp.bfloat16)
    got_lower_2 = swap(lower_2, "row", 2)
    across = swap(act, "col", 2)
    pair = jnp.where(x == 0, jnp.stack([act, across]), jnp.stack([across, act]))
    pair = pair.reshape(2 * quarter, length)
    other = swap(pair, "col", 1)
    whole = jnp.where(core == 0, jnp.stack([pair, other]), jnp.stack([other, pair]))
    whole = whole.reshape(4 * quarter, length)
    got_second = jnp.concatenate([got_upper_2, got_lower_2])
    grad = own + unpack(got_first, GRAD_UP) + unpack(got_second, GRAD_UP)
    tile, to_3, to_2, to_1 = make_tile(order, token_ids, whole, grad.astype(jnp.bfloat16))
    from_3, from_2, from_1 = swap(to_3, "row", 3), swap(to_2, "row", 2), swap(to_1, "row", 1)
    return (
        tile
        + from_3.astype(jnp.float32)
        + from_2.astype(jnp.float32)
        + from_1.astype(jnp.float32)
    )


def solution(mesh):
    in_specs = (
        P("groups", ("row", "col")),
        P(("groups", "row", "col"), None),
        P("groups", "row"),
        P(("groups", "row"), "col"),
        P(),
    )
    out_specs = P(("groups", "row"), "col")
    rows, columns = mesh.shape["row"], mesh.shape["col"]

    def shards(*arrays):
        fits = rows == 4 and columns == 4 and arrays[4].shape[0] == rows
        return (line_shards if fits else plain_shards)(*arrays)

    return jax.shard_map(shards, mesh=mesh, in_specs=in_specs, out_specs=out_specs, check_vma=False)
```

```python
import jax
import jax.numpy as jnp
from jax import lax
from jax.experimental import pallas as pl
from jax.experimental.pallas import tpu as pltpu
from jax.sharding import PartitionSpec as P

VMEM = pl.BlockSpec(memory_space=pltpu.VMEM)
SMEM = pl.BlockSpec(memory_space=pltpu.SMEM)
HBM = pl.BlockSpec(memory_space=pltpu.HBM)
ACT_UP = 4.0
GRAD_UP = 8.0
CUT = 1024


def plain_shards(activations, basis_in, gradients, basis_out, token_ids):
    sequences = token_ids.shape[0]
    keep_mask = (token_ids != 0).astype(jnp.float32)
    counts = jnp.sum(keep_mask, axis=1)
    scales = 1.0 / jnp.sqrt(counts)
    flat_keep = keep_mask.reshape(1, -1).astype(jnp.bfloat16)
    act_share = lax.psum_scatter(
        lax.dot_general(
            basis_in, activations, (((0,), (1,)), ((), ())), preferred_element_type=jnp.float32
        ),
        ("row", "col"),
        scatter_dimension=0,
        tiled=True,
    ).astype(jnp.bfloat16)
    act_local = lax.all_gather(act_share, "col", axis=0, tiled=True) * flat_keep
    partial_value = jnp.dot(gradients, basis_out, preferred_element_type=jnp.float32)
    rot_grad = lax.psum(partial_value, "row").astype(jnp.bfloat16)
    height = act_local.shape[0]
    width = rot_grad.shape[1]
    act_blocks = act_local.reshape(height, sequences, -1)
    grad_blocks = rot_grad.reshape(sequences, -1, width)
    products = jnp.einsum(
        "rsl,slc->rsc", act_blocks, grad_blocks, preferred_element_type=jnp.float32
    )
    products = products * scales[None, :, None]
    return jnp.mean(products * products, axis=1)


def in_hbm(value):
    return pltpu.with_memory_space_constraint(value, pltpu.HBM)


def columns_by_rows(weights, rows):
    return lax.dot_general(
        weights, rows, (((0,), (1,)), ((), ())), preferred_element_type=jnp.float32
    )


def pieces(depth):
    return [(at, min(CUT, depth - at)) for at in range(0, depth, CUT)]


def fetch_block(block, gradients, buffer, sems):
    length, depth = buffer.shape
    start = pl.multiple_of(block * length, length)
    return [
        pltpu.make_async_copy(
            gradients.at[pl.ds(start, length), pl.ds(at, size)],
            buffer.at[:, pl.ds(at, size)],
            sems.at[i],
        )
        for i, (at, size) in enumerate(pieces(depth))
    ]


def rotate_block(copies, weights, buffer, out):
    edges = pieces(buffer.shape[1])
    for i, (at, size) in enumerate(edges):
        for copy in copies[i]:
            copy.wait()
        part = columns_by_rows(weights[at : at + size, :], buffer[:, at : at + size])
        if i == 0:
            out[...] = part
        else:
            out[...] += part


def grad_kernel(block, gradients, basis, out, weights, buffer, grad_sems, basis_sems):
    copies = []
    edges = pieces(buffer.shape[1])
    for i, copy in enumerate(fetch_block(block[0], gradients, buffer, grad_sems)):
        at, size = edges[i]
        part = pltpu.make_async_copy(
            basis.at[pl.ds(at, size), :], weights.at[pl.ds(at, size), :], basis_sems.at[i]
        )
        part.start()
        copy.start()
        copies.append((part, copy))
    rotate_block(copies, weights, buffer, out)


def rotate_grad(block, gradients, basis_out, length):
    depth, width = basis_out.shape
    steps = len(pieces(depth))
    return pl.pallas_call(
        grad_kernel,
        in_specs=[SMEM, HBM, HBM],
        out_specs=VMEM,
        out_shape=jax.ShapeDtypeStruct((width, length), jnp.float32),
        scratch_shapes=[
            pltpu.VMEM((depth, width), basis_out.dtype),
            pltpu.VMEM((length, depth), jnp.bfloat16),
            pltpu.SemaphoreType.DMA((steps,)),
            pltpu.SemaphoreType.DMA((steps,)),
        ],
        compiler_params=pltpu.CompilerParams(vmem_limit_bytes=14 * 2**20),
        cost_estimate=pl.CostEstimate(
            flops=2 * length * depth * width,
            bytes_accessed=2 * depth * (length + width),
            transcendentals=0,
        ),
    )(jnp.reshape(block, (1,)), in_hbm(gradients), in_hbm(basis_out))


def act_kernel(where, act, basis, far_act, far_basis, *outs):
    quarter, length = outs[0].shape
    z, core, x = where[0], where[1], where[2]
    span = pl.ds(pl.multiple_of(core * 2 * quarter, 2 * quarter), 2 * quarter)
    near = basis[:, span]
    far = far_basis[:, span]
    for i, step in enumerate((3, 2, 1, 0)):
        rows = pl.ds(pl.multiple_of((z ^ step) * length, length), length)
        product = columns_by_rows(near, act[rows, :]) + columns_by_rows(far, far_act[rows, :])
        low, high = product[:quarter], product[quarter:]
        outs[2 * i][...] = jnp.where(x == 0, low, high)
        outs[2 * i + 1][...] = jnp.where(x == 0, high, low)


def rotate_act(where, activations, basis_in, far_act, far_basis, length):
    shape = jax.ShapeDtypeStruct((basis_in.shape[1] // 4, length), jnp.float32)
    return pl.pallas_call(
        act_kernel,
        in_specs=[SMEM, VMEM, VMEM, VMEM, VMEM],
        out_specs=[VMEM] * 8,
        out_shape=[shape] * 8,
        compiler_params=pltpu.CompilerParams(vmem_limit_bytes=6 * 2**20),
        cost_estimate=pl.CostEstimate(
            flops=2 * activations.size * basis_in.shape[1],
            bytes_accessed=4 * activations.size,
            transcendentals=0,
        ),
    )(where, activations, basis_in, far_act, far_basis)


def tile_kernel(order, ids, act, grad, own, *sends):
    sequences, rows = ids.shape[0], own.shape[0]
    keep = (ids[pl.ds(order[0], 1), :] != 0).astype(jnp.float32)
    weight = 1.0 / jnp.sqrt(jnp.sum(keep, axis=1, keepdims=True))
    keep = keep.astype(jnp.bfloat16)
    for slot, out in enumerate((own, *sends)):
        piece = act[pl.ds(pl.multiple_of(order[slot] * rows, rows), rows), :] * keep
        product = lax.dot_general(
            piece, grad[...], (((1,), (1,)), ((), ())), preferred_element_type=jnp.float32
        )
        product = product * weight
        out[...] = (product * product * (1.0 / sequences)).astype(out.dtype)


def make_tile(order, token_ids, act, grad):
    sequences = token_ids.shape[0]
    rows, width = act.shape[0] // sequences, grad.shape[0]
    return pl.pallas_call(
        tile_kernel,
        in_specs=[SMEM, VMEM, VMEM, VMEM],
        out_specs=[VMEM] * sequences,
        out_shape=[jax.ShapeDtypeStruct((rows, width), jnp.float32)]
        + [jax.ShapeDtypeStruct((rows, width), jnp.bfloat16)] * (sequences - 1),
        compiler_params=pltpu.CompilerParams(vmem_limit_bytes=16 * 2**20),
        cost_estimate=pl.CostEstimate(flops=1, bytes_accessed=1, transcendentals=0),
    )(order, token_ids, act, grad)


def swap(value, axis, step, size=4):
    return lax.ppermute(value, axis, [(i, i ^ step) for i in range(size)])


def pack(value, up):
    return (value * up).astype(jnp.float16)


def unpack(value, up):
    return value.astype(jnp.float32) * (1.0 / up)


def line_shards(activations, basis_in, gradients, basis_out, token_ids):
    length = token_ids.shape[1]
    z = lax.axis_index("row").astype(jnp.int32)
    place = lax.axis_index("col").astype(jnp.int32)
    core, x = place & 1, place >> 1
    quarter = basis_in.shape[1] // 4
    middle = basis_out.shape[1] // 2
    tie = lax.optimization_barrier
    order = jnp.stack([z, z ^ 2, z ^ 3, z ^ 1])
    where = jnp.stack([z, core, x])

    far_act, far_basis = swap(activations, "col", 1), swap(basis_in, "col", 1)
    third = rotate_grad(z ^ 3, gradients, basis_out, length)
    third = pack(third, GRAD_UP)
    got_third = swap(third, "row", 1)

    far_act, far_basis, third, order = tie((far_act, far_basis, third, order))
    mine_3, other_3, mine_2, other_2, mine_1, other_1, mine_0, other_0 = rotate_act(
        where, activations, basis_in, far_act, far_basis, length
    )
    out_3 = pack(other_3, ACT_UP)
    out_210 = pack(jnp.stack([other_2, other_1, other_0]), ACT_UP)
    got_3 = swap(out_3, "col", 2)
    got_210 = swap(out_210, "col", 2)

    block, out_3, out_210 = tie((z ^ 2, out_3, out_210))
    second = rotate_grad(block, gradients, basis_out, length)
    got_third, second = tie((got_third, second))
    second = second + unpack(got_third, GRAD_UP)
    upper_2, lower_2 = pack(second[:middle], GRAD_UP), pack(second[middle:], GRAD_UP)
    got_upper_2 = swap(upper_2, "row", 2)
    got_3, upper_2 = tie((got_3, upper_2))
    act_3 = pack(mine_3 + unpack(got_3, ACT_UP), ACT_UP)
    over_3 = swap(act_3, "row", 1)

    block, act_3, upper_2 = tie((z ^ 1, act_3, upper_2))
    first = rotate_grad(block, gradients, basis_out, length)
    got_210, over_3, first = tie((got_210, over_3, first))
    act_2 = pack(mine_2 + unpack(got_210[0], ACT_UP) + unpack(over_3, ACT_UP), ACT_UP)
    over_2 = swap(act_2, "row", 2)
    act_1 = pack(mine_1 + unpack(got_210[1], ACT_UP), ACT_UP)
    act_0 = mine_0 + unpack(got_210[2], ACT_UP)
    over_1 = swap(act_1, "row", 1)
    first, act_2, act_1, act_0 = tie((first, act_2, act_1, act_0))
    first_out = pack(first, GRAD_UP)
    got_first = swap(first_out, "row", 1)
    block, first_out = tie((z, first_out))
    own = rotate_grad(block, gradients, basis_out, length)
    over_1, over_2, got_upper_2, own = tie((over_1, over_2, got_upper_2, own))
    act = act_0 + unpack(over_1, ACT_UP) + unpack(over_2, ACT_UP)
    act = act.astype(jnp.bfloat16)
    got_lower_2 = swap(lower_2, "row", 2)
    across = swap(act, "col", 2)
    pair = jnp.where(x == 0, jnp.stack([act, across]), jnp.stack([across, act]))
    pair = pair.reshape(2 * quarter, length)
    other = swap(pair, "col", 1)
    whole = jnp.where(core == 0, jnp.stack([pair, other]), jnp.stack([other, pair]))
    whole = whole.reshape(4 * quarter, length)
    got_second = jnp.concatenate([got_upper_2, got_lower_2])
    grad = own + unpack(got_first, GRAD_UP) + unpack(got_second, GRAD_UP)
    tile, to_2, to_3, to_1 = make_tile(order, token_ids, whole, grad.astype(jnp.bfloat16))
    from_2 = swap(to_2, "row", 2)
    from_3 = swap(to_3, "row", 3)
    from_1 = swap(to_1, "row", 1)
    return (
        tile
        + from_2.astype(jnp.float32)
        + from_3.astype(jnp.float32)
        + from_1.astype(jnp.float32)
    )


def solution(mesh):
    in_specs = (
        P("groups", ("row", "col")),
        P(("groups", "row", "col"), None),
        P("groups", "row"),
        P(("groups", "row"), "col"),
        P(),
    )
    out_specs = P(("groups", "row"), "col")
    rows, columns = mesh.shape["row"], mesh.shape["col"]

    def shards(*arrays):
        fits = rows == 4 and columns == 4 and arrays[4].shape[0] == rows
        return (line_shards if fits else plain_shards)(*arrays)

    return jax.shard_map(shards, mesh=mesh, in_specs=in_specs, out_specs=out_specs, check_vma=False)
```

```python
import jax
import jax.numpy as jnp
from jax import lax
from jax.experimental import pallas as pl
from jax.experimental.pallas import tpu as pltpu
from jax.sharding import PartitionSpec as P

VMEM = pl.BlockSpec(memory_space=pltpu.VMEM)
SMEM = pl.BlockSpec(memory_space=pltpu.SMEM)
HBM = pl.BlockSpec(memory_space=pltpu.HBM)
ACT_UP = 4.0
GRAD_UP = 8.0
CUT = 1024


def plain_shards(activations, basis_in, gradients, basis_out, token_ids):
    sequences = token_ids.shape[0]
    keep_mask = (token_ids != 0).astype(jnp.float32)
    counts = jnp.sum(keep_mask, axis=1)
    scales = 1.0 / jnp.sqrt(counts)
    flat_keep = keep_mask.reshape(1, -1).astype(jnp.bfloat16)
    act_share = lax.psum_scatter(
        lax.dot_general(
            basis_in, activations, (((0,), (1,)), ((), ())), preferred_element_type=jnp.float32
        ),
        ("row", "col"),
        scatter_dimension=0,
        tiled=True,
    ).astype(jnp.bfloat16)
    act_local = lax.all_gather(act_share, "col", axis=0, tiled=True) * flat_keep
    partial_value = jnp.dot(gradients, basis_out, preferred_element_type=jnp.float32)
    rot_grad = lax.psum(partial_value, "row").astype(jnp.bfloat16)
    height = act_local.shape[0]
    width = rot_grad.shape[1]
    act_blocks = act_local.reshape(height, sequences, -1)
    grad_blocks = rot_grad.reshape(sequences, -1, width)
    products = jnp.einsum(
        "rsl,slc->rsc", act_blocks, grad_blocks, preferred_element_type=jnp.float32
    )
    products = products * scales[None, :, None]
    return jnp.mean(products * products, axis=1)


def in_hbm(value):
    return pltpu.with_memory_space_constraint(value, pltpu.HBM)


def columns_by_rows(weights, rows):
    return lax.dot_general(
        weights, rows, (((0,), (1,)), ((), ())), preferred_element_type=jnp.float32
    )


def pieces(depth):
    return [(at, min(CUT, depth - at)) for at in range(0, depth, CUT)]


def fetch_block(block, gradients, buffer, sems):
    length, depth = buffer.shape
    start = pl.multiple_of(block * length, length)
    return [
        pltpu.make_async_copy(
            gradients.at[pl.ds(start, length), pl.ds(at, size)],
            buffer.at[:, pl.ds(at, size)],
            sems.at[i],
        )
        for i, (at, size) in enumerate(pieces(depth))
    ]


def rotate_block(copies, weights, buffer, out):
    edges = pieces(buffer.shape[1])
    for i, (at, size) in enumerate(edges):
        for copy in copies[i]:
            copy.wait()
        part = columns_by_rows(weights[at : at + size, :], buffer[:, at : at + size])
        if i == 0:
            out[...] = part
        else:
            out[...] += part


def grad_kernel(block, gradients, basis, out, weights, buffer, grad_sems, basis_sems):
    copies = []
    edges = pieces(buffer.shape[1])
    for i, copy in enumerate(fetch_block(block[0], gradients, buffer, grad_sems)):
        at, size = edges[i]
        part = pltpu.make_async_copy(
            basis.at[pl.ds(at, size), :], weights.at[pl.ds(at, size), :], basis_sems.at[i]
        )
        part.start()
        copy.start()
        copies.append((part, copy))
    rotate_block(copies, weights, buffer, out)


def rotate_grad(block, gradients, basis_out, length):
    depth, width = basis_out.shape
    steps = len(pieces(depth))
    return pl.pallas_call(
        grad_kernel,
        in_specs=[SMEM, HBM, HBM],
        out_specs=VMEM,
        out_shape=jax.ShapeDtypeStruct((width, length), jnp.float32),
        scratch_shapes=[
            pltpu.VMEM((depth, width), basis_out.dtype),
            pltpu.VMEM((length, depth), jnp.bfloat16),
            pltpu.SemaphoreType.DMA((steps,)),
            pltpu.SemaphoreType.DMA((steps,)),
        ],
        compiler_params=pltpu.CompilerParams(vmem_limit_bytes=14 * 2**20),
        cost_estimate=pl.CostEstimate(
            flops=2 * length * depth * width,
            bytes_accessed=2 * depth * (length + width),
            transcendentals=0,
        ),
    )(jnp.reshape(block, (1,)), in_hbm(gradients), in_hbm(basis_out))


def act_kernel(where, act, basis, far_act, far_basis, *outs):
    quarter, length = outs[0].shape
    z, core, x = where[0], where[1], where[2]
    span = pl.ds(pl.multiple_of(core * 2 * quarter, 2 * quarter), 2 * quarter)
    near = basis[:, span]
    far = far_basis[:, span]
    for i, step in enumerate((3, 2, 1, 0)):
        rows = pl.ds(pl.multiple_of((z ^ step) * length, length), length)
        product = columns_by_rows(near, act[rows, :]) + columns_by_rows(far, far_act[rows, :])
        low, high = product[:quarter], product[quarter:]
        outs[2 * i][...] = jnp.where(x == 0, low, high)
        outs[2 * i + 1][...] = jnp.where(x == 0, high, low)


def rotate_act(where, activations, basis_in, far_act, far_basis, length):
    shape = jax.ShapeDtypeStruct((basis_in.shape[1] // 4, length), jnp.float32)
    return pl.pallas_call(
        act_kernel,
        in_specs=[SMEM, VMEM, VMEM, VMEM, VMEM],
        out_specs=[VMEM] * 8,
        out_shape=[shape] * 8,
        compiler_params=pltpu.CompilerParams(vmem_limit_bytes=6 * 2**20),
        cost_estimate=pl.CostEstimate(
            flops=2 * activations.size * basis_in.shape[1],
            bytes_accessed=4 * activations.size,
            transcendentals=0,
        ),
    )(where, activations, basis_in, far_act, far_basis)


def tile_kernel(order, ids, act, grad, own, *sends):
    sequences, rows = ids.shape[0], own.shape[0]
    keep = (ids[pl.ds(order[0], 1), :] != 0).astype(jnp.float32)
    weight = 1.0 / jnp.sqrt(jnp.sum(keep, axis=1, keepdims=True))
    keep = keep.astype(jnp.bfloat16)
    for slot, out in enumerate((own, *sends)):
        piece = act[pl.ds(pl.multiple_of(order[slot] * rows, rows), rows), :] * keep
        product = lax.dot_general(
            piece, grad[...], (((1,), (1,)), ((), ())), preferred_element_type=jnp.float32
        )
        product = product * weight
        out[...] = (product * product * (1.0 / sequences)).astype(out.dtype)


def make_tile(order, token_ids, act, grad):
    sequences = token_ids.shape[0]
    rows, width = act.shape[0] // sequences, grad.shape[0]
    return pl.pallas_call(
        tile_kernel,
        in_specs=[SMEM, VMEM, VMEM, VMEM],
        out_specs=[VMEM] * sequences,
        out_shape=[jax.ShapeDtypeStruct((rows, width), jnp.float32)]
        + [jax.ShapeDtypeStruct((rows, width), jnp.bfloat16)] * (sequences - 1),
        compiler_params=pltpu.CompilerParams(vmem_limit_bytes=16 * 2**20),
        cost_estimate=pl.CostEstimate(flops=1, bytes_accessed=1, transcendentals=0),
    )(order, token_ids, act, grad)


def swap(value, axis, step, size=4):
    return lax.ppermute(value, axis, [(i, i ^ step) for i in range(size)])


def pack(value, up):
    return (value * up).astype(jnp.float16)


def unpack(value, up):
    return value.astype(jnp.float32) * (1.0 / up)


def line_shards(activations, basis_in, gradients, basis_out, token_ids):
    length = token_ids.shape[1]
    z = lax.axis_index("row").astype(jnp.int32)
    place = lax.axis_index("col").astype(jnp.int32)
    core, x = place & 1, place >> 1
    quarter = basis_in.shape[1] // 4
    middle = basis_out.shape[1] // 2
    tie = lax.optimization_barrier
    order = jnp.stack([z, z ^ 2, z ^ 3, z ^ 1])
    where = jnp.stack([z, core, x])

    far_act, far_basis = swap(activations, "col", 1), swap(basis_in, "col", 1)
    third = rotate_grad(z ^ 3, gradients, basis_out, length)
    third = pack(third, GRAD_UP)
    got_third = swap(third, "row", 1)

    far_act, far_basis, third, order = tie((far_act, far_basis, third, order))
    mine_3, other_3, mine_2, other_2, mine_1, other_1, mine_0, other_0 = rotate_act(
        where, activations, basis_in, far_act, far_basis, length
    )
    out_3 = pack(other_3, ACT_UP)
    out_210 = pack(jnp.stack([other_2, other_1, other_0]), ACT_UP)
    got_3 = swap(out_3, "col", 2)
    got_210 = swap(out_210, "col", 2)

    block, out_3, out_210 = tie((z ^ 2, out_3, out_210))
    second = rotate_grad(block, gradients, basis_out, length)
    got_third, second = tie((got_third, second))
    upper_2 = pack(second[:middle] + unpack(got_third[:middle], GRAD_UP), GRAD_UP)
    got_upper_2 = swap(upper_2, "row", 2)
    got_third, second, upper_2 = tie((got_third, second, upper_2))
    got_3, upper_2 = tie((got_3, upper_2))
    act_3 = pack(mine_3 + unpack(got_3, ACT_UP), ACT_UP)
    over_3 = swap(act_3, "row", 1)

    block, act_3, upper_2 = tie((z ^ 1, act_3, upper_2))
    first = rotate_grad(block, gradients, basis_out, length)
    got_210, over_3, first = tie((got_210, over_3, first))
    act_2 = pack(mine_2 + unpack(got_210[0], ACT_UP) + unpack(over_3, ACT_UP), ACT_UP)
    over_2 = swap(act_2, "row", 2)
    act_1 = pack(mine_1 + unpack(got_210[1], ACT_UP), ACT_UP)
    act_0 = mine_0 + unpack(got_210[2], ACT_UP)
    over_1 = swap(act_1, "row", 1)
    first, act_2, act_1, act_0 = tie((first, act_2, act_1, act_0))
    first_out = pack(first, GRAD_UP)
    got_first = swap(first_out, "row", 1)
    got_third, first_out = tie((got_third, first_out))
    lower_2 = pack(second[middle:] + unpack(got_third[middle:], GRAD_UP), GRAD_UP)
    block, first_out, lower_2 = tie((z, first_out, lower_2))
    own = rotate_grad(block, gradients, basis_out, length)
    over_1, over_2, got_upper_2, own = tie((over_1, over_2, got_upper_2, own))
    act = act_0 + unpack(over_1, ACT_UP) + unpack(over_2, ACT_UP)
    act = act.astype(jnp.bfloat16)
    got_lower_2 = swap(lower_2, "row", 2)
    across = swap(act, "col", 2)
    pair = jnp.where(x == 0, jnp.stack([act, across]), jnp.stack([across, act]))
    pair = pair.reshape(2 * quarter, length)
    other = swap(pair, "col", 1)
    whole = jnp.where(core == 0, jnp.stack([pair, other]), jnp.stack([other, pair]))
    whole = whole.reshape(4 * quarter, length)
    got_second = jnp.concatenate([got_upper_2, got_lower_2])
    grad = own + unpack(got_first, GRAD_UP) + unpack(got_second, GRAD_UP)
    tile, to_2, to_3, to_1 = make_tile(order, token_ids, whole, grad.astype(jnp.bfloat16))
    from_2 = swap(to_2, "row", 2)
    from_3 = swap(to_3, "row", 3)
    from_1 = swap(to_1, "row", 1)
    return (
        tile
        + from_2.astype(jnp.float32)
        + from_3.astype(jnp.float32)
        + from_1.astype(jnp.float32)
    )


def solution(mesh):
    in_specs = (
        P("groups", ("row", "col")),
        P(("groups", "row", "col"), None),
        P("groups", "row"),
        P(("groups", "row"), "col"),
        P(),
    )
    out_specs = P(("groups", "row"), "col")
    rows, columns = mesh.shape["row"], mesh.shape["col"]

    def shards(*arrays):
        fits = rows == 4 and columns == 4 and arrays[4].shape[0] == rows
        return (line_shards if fits else plain_shards)(*arrays)

    return jax.shard_map(shards, mesh=mesh, in_specs=in_specs, out_specs=out_specs, check_vma=False)
```

```python
import jax
import jax.numpy as jnp
from jax import lax
from jax.experimental import pallas as pl
from jax.experimental.pallas import tpu as pltpu
from jax.sharding import PartitionSpec as P

VMEM = pl.BlockSpec(memory_space=pltpu.VMEM)
SMEM = pl.BlockSpec(memory_space=pltpu.SMEM)
HBM = pl.BlockSpec(memory_space=pltpu.HBM)
ACT_UP = 4.0
GRAD_UP = 8.0
CUT = 1024


def plain_shards(activations, basis_in, gradients, basis_out, token_ids):
    sequences = token_ids.shape[0]
    keep_mask = (token_ids != 0).astype(jnp.float32)
    counts = jnp.sum(keep_mask, axis=1)
    scales = 1.0 / jnp.sqrt(counts)
    flat_keep = keep_mask.reshape(1, -1).astype(jnp.bfloat16)
    act_share = lax.psum_scatter(
        lax.dot_general(
            basis_in, activations, (((0,), (1,)), ((), ())), preferred_element_type=jnp.float32
        ),
        ("row", "col"),
        scatter_dimension=0,
        tiled=True,
    ).astype(jnp.bfloat16)
    act_local = lax.all_gather(act_share, "col", axis=0, tiled=True) * flat_keep
    partial_value = jnp.dot(gradients, basis_out, preferred_element_type=jnp.float32)
    rot_grad = lax.psum(partial_value, "row").astype(jnp.bfloat16)
    height = act_local.shape[0]
    width = rot_grad.shape[1]
    act_blocks = act_local.reshape(height, sequences, -1)
    grad_blocks = rot_grad.reshape(sequences, -1, width)
    products = jnp.einsum(
        "rsl,slc->rsc", act_blocks, grad_blocks, preferred_element_type=jnp.float32
    )
    products = products * scales[None, :, None]
    return jnp.mean(products * products, axis=1)


def in_hbm(value):
    return pltpu.with_memory_space_constraint(value, pltpu.HBM)


def columns_by_rows(weights, rows):
    return lax.dot_general(
        weights, rows, (((0,), (1,)), ((), ())), preferred_element_type=jnp.float32
    )


def pieces(depth):
    return [(at, min(CUT, depth - at)) for at in range(0, depth, CUT)]


def fetch_block(block, gradients, buffer, sems):
    length, depth = buffer.shape
    start = pl.multiple_of(block * length, length)
    return [
        pltpu.make_async_copy(
            gradients.at[pl.ds(start, length), pl.ds(at, size)],
            buffer.at[:, pl.ds(at, size)],
            sems.at[i],
        )
        for i, (at, size) in enumerate(pieces(depth))
    ]


def rotate_block(copies, weights, buffer, out):
    edges = pieces(buffer.shape[1])
    for i, (at, size) in enumerate(edges):
        for copy in copies[i]:
            copy.wait()
        part = columns_by_rows(weights[at : at + size, :], buffer[:, at : at + size])
        if i == 0:
            out[...] = part
        else:
            out[...] += part


def grad_kernel(block, gradients, basis, out, weights, buffer, grad_sems, basis_sems):
    copies = []
    edges = pieces(buffer.shape[1])
    for i, copy in enumerate(fetch_block(block[0], gradients, buffer, grad_sems)):
        at, size = edges[i]
        part = pltpu.make_async_copy(
            basis.at[pl.ds(at, size), :], weights.at[pl.ds(at, size), :], basis_sems.at[i]
        )
        part.start()
        copy.start()
        copies.append((part, copy))
    rotate_block(copies, weights, buffer, out)


def rotate_grad(block, gradients, basis_out, length):
    depth, width = basis_out.shape
    steps = len(pieces(depth))
    return pl.pallas_call(
        grad_kernel,
        in_specs=[SMEM, HBM, HBM],
        out_specs=VMEM,
        out_shape=jax.ShapeDtypeStruct((width, length), jnp.float32),
        scratch_shapes=[
            pltpu.VMEM((depth, width), basis_out.dtype),
            pltpu.VMEM((length, depth), jnp.bfloat16),
            pltpu.SemaphoreType.DMA((steps,)),
            pltpu.SemaphoreType.DMA((steps,)),
        ],
        compiler_params=pltpu.CompilerParams(vmem_limit_bytes=14 * 2**20),
        cost_estimate=pl.CostEstimate(
            flops=2 * length * depth * width,
            bytes_accessed=2 * depth * (length + width),
            transcendentals=0,
        ),
    )(jnp.reshape(block, (1,)), in_hbm(gradients), in_hbm(basis_out))


def act_kernel(where, act, basis, far_act, far_basis, *outs):
    quarter, length = outs[0].shape
    z, core, x = where[0], where[4], where[5]
    span = pl.ds(pl.multiple_of(core * 2 * quarter, 2 * quarter), 2 * quarter)
    near = basis[:, span]
    far = far_basis[:, span]
    for i, step in enumerate((3, 2, 1, 0)):
        rows = pl.ds(pl.multiple_of((z ^ step) * length, length), length)
        product = columns_by_rows(near, act[rows, :]) + columns_by_rows(far, far_act[rows, :])
        low, high = product[:quarter], product[quarter:]
        outs[2 * i][...] = jnp.where(x == 0, low, high)
        outs[2 * i + 1][...] = jnp.where(x == 0, high, low)


def rotate_act(where, activations, basis_in, far_act, far_basis, length):
    shape = jax.ShapeDtypeStruct((basis_in.shape[1] // 4, length), jnp.float32)
    return pl.pallas_call(
        act_kernel,
        in_specs=[SMEM, VMEM, VMEM, VMEM, VMEM],
        out_specs=[VMEM] * 8,
        out_shape=[shape] * 8,
        compiler_params=pltpu.CompilerParams(vmem_limit_bytes=6 * 2**20),
        cost_estimate=pl.CostEstimate(
            flops=2 * activations.size * basis_in.shape[1],
            bytes_accessed=4 * activations.size,
            transcendentals=0,
        ),
    )(where, activations, basis_in, far_act, far_basis)


def tile_kernel(order, ids, act, grad, own, *sends):
    sequences, rows = ids.shape[0], own.shape[0]
    keep = (ids[pl.ds(order[0], 1), :] != 0).astype(jnp.float32)
    weight = 1.0 / jnp.sqrt(jnp.sum(keep, axis=1, keepdims=True))
    keep = keep.astype(jnp.bfloat16)
    for slot, out in enumerate((own, *sends)):
        piece = act[pl.ds(pl.multiple_of(order[slot] * rows, rows), rows), :] * keep
        product = lax.dot_general(
            piece, grad[...], (((1,), (1,)), ((), ())), preferred_element_type=jnp.float32
        )
        product = product * weight
        out[...] = (product * product * (1.0 / sequences)).astype(out.dtype)


def make_tile(order, token_ids, act, grad):
    sequences = token_ids.shape[0]
    rows, width = act.shape[0] // sequences, grad.shape[0]
    return pl.pallas_call(
        tile_kernel,
        in_specs=[SMEM, VMEM, VMEM, VMEM],
        out_specs=[VMEM] * sequences,
        out_shape=[jax.ShapeDtypeStruct((rows, width), jnp.float32)]
        + [jax.ShapeDtypeStruct((rows, width), jnp.bfloat16)] * (sequences - 1),
        compiler_params=pltpu.CompilerParams(vmem_limit_bytes=16 * 2**20),
        cost_estimate=pl.CostEstimate(flops=1, bytes_accessed=1, transcendentals=0),
    )(order, token_ids, act, grad)


def swap(value, axis, step, size=4):
    return lax.ppermute(value, axis, [(i, i ^ step) for i in range(size)])


def pack(value, up):
    return (value * up).astype(jnp.float16)


def unpack(value, up):
    return value.astype(jnp.float32) * (1.0 / up)


def line_shards(activations, basis_in, gradients, basis_out, token_ids):
    length = token_ids.shape[1]
    z = lax.axis_index("row").astype(jnp.int32)
    place = lax.axis_index("col").astype(jnp.int32)
    core, x = place & 1, place >> 1
    quarter = basis_in.shape[1] // 4
    middle = basis_out.shape[1] // 2
    tie = lax.optimization_barrier
    order = jnp.stack([z, z ^ 2, z ^ 3, z ^ 1, core, x])

    far_act, far_basis = swap(activations, "col", 1), swap(basis_in, "col", 1)
    third = rotate_grad(z ^ 3, gradients, basis_out, length)
    third = pack(third, GRAD_UP)
    got_third = swap(third, "row", 1)

    far_act, far_basis, third, order = tie((far_act, far_basis, third, order))
    mine_3, other_3, mine_2, other_2, mine_1, other_1, mine_0, other_0 = rotate_act(
        order, activations, basis_in, far_act, far_basis, length
    )
    out_3 = pack(other_3, ACT_UP)
    out_210 = pack(jnp.stack([other_2, other_1, other_0]), ACT_UP)
    got_3 = swap(out_3, "col", 2)
    got_210 = swap(out_210, "col", 2)

    block, out_3, out_210 = tie((z ^ 2, out_3, out_210))
    second = rotate_grad(block, gradients, basis_out, length)
    got_third, second = tie((got_third, second))
    upper_2 = pack(second[:middle] + unpack(got_third[:middle], GRAD_UP), GRAD_UP)
    got_upper_2 = swap(upper_2, "row", 2)
    got_third, second, upper_2 = tie((got_third, second, upper_2))
    got_3, upper_2 = tie((got_3, upper_2))
    act_3 = pack(mine_3 + unpack(got_3, ACT_UP), ACT_UP)
    over_3 = swap(act_3, "row", 1)

    block, act_3, upper_2 = tie((z ^ 1, act_3, upper_2))
    first = rotate_grad(block, gradients, basis_out, length)
    got_210, over_3, first = tie((got_210, over_3, first))
    act_2 = pack(mine_2 + unpack(got_210[0], ACT_UP) + unpack(over_3, ACT_UP), ACT_UP)
    over_2 = swap(act_2, "row", 2)
    act_1 = pack(mine_1 + unpack(got_210[1], ACT_UP), ACT_UP)
    act_0 = mine_0 + unpack(got_210[2], ACT_UP)
    over_1 = swap(act_1, "row", 1)
    first, act_2, act_1, act_0 = tie((first, act_2, act_1, act_0))
    first_out = pack(first, GRAD_UP)
    got_first = swap(first_out, "row", 1)
    got_third, first_out = tie((got_third, first_out))
    lower_2 = pack(second[middle:] + unpack(got_third[middle:], GRAD_UP), GRAD_UP)
    block, first_out, lower_2 = tie((z, first_out, lower_2))
    own = rotate_grad(block, gradients, basis_out, length)
    over_1, over_2, got_upper_2, own = tie((over_1, over_2, got_upper_2, own))
    act = act_0 + unpack(over_1, ACT_UP) + unpack(over_2, ACT_UP)
    act = act.astype(jnp.bfloat16)
    got_lower_2 = swap(lower_2, "row", 2)
    across = swap(act, "col", 2)
    pair = jnp.where(x == 0, jnp.stack([act, across]), jnp.stack([across, act]))
    pair = pair.reshape(2 * quarter, length)
    other = swap(pair, "col", 1)
    whole = jnp.where(core == 0, jnp.stack([pair, other]), jnp.stack([other, pair]))
    whole = whole.reshape(4 * quarter, length)
    got_second = jnp.concatenate([got_upper_2, got_lower_2])
    grad = own + unpack(got_first, GRAD_UP) + unpack(got_second, GRAD_UP)
    tile, to_2, to_3, to_1 = make_tile(order, token_ids, whole, grad.astype(jnp.bfloat16))
    from_2 = swap(to_2, "row", 2)
    from_3 = swap(to_3, "row", 3)
    from_1 = swap(to_1, "row", 1)
    return (
        tile
        + from_2.astype(jnp.float32)
        + from_3.astype(jnp.float32)
        + from_1.astype(jnp.float32)
    )


def solution(mesh):
    in_specs = (
        P("groups", ("row", "col")),
        P(("groups", "row", "col"), None),
        P("groups", "row"),
        P(("groups", "row"), "col"),
        P(),
    )
    out_specs = P(("groups", "row"), "col")
    rows, columns = mesh.shape["row"], mesh.shape["col"]

    def shards(*arrays):
        fits = rows == 4 and columns == 4 and arrays[4].shape[0] == rows
        return (line_shards if fits else plain_shards)(*arrays)

    return jax.shard_map(shards, mesh=mesh, in_specs=in_specs, out_specs=out_specs, check_vma=False)
```

```python
import jax
import jax.numpy as jnp
from jax import lax
from jax.experimental import pallas as pl
from jax.experimental.pallas import tpu as pltpu
from jax.sharding import PartitionSpec as P

VMEM = pl.BlockSpec(memory_space=pltpu.VMEM)
SMEM = pl.BlockSpec(memory_space=pltpu.SMEM)
HBM = pl.BlockSpec(memory_space=pltpu.HBM)
ACT_UP = 4.0
GRAD_UP = 8.0
CUT = 1024


def plain_shards(activations, basis_in, gradients, basis_out, token_ids):
    sequences = token_ids.shape[0]
    keep_mask = (token_ids != 0).astype(jnp.float32)
    counts = jnp.sum(keep_mask, axis=1)
    scales = 1.0 / jnp.sqrt(counts)
    flat_keep = keep_mask.reshape(1, -1).astype(jnp.bfloat16)
    act_share = lax.psum_scatter(
        lax.dot_general(
            basis_in, activations, (((0,), (1,)), ((), ())), preferred_element_type=jnp.float32
        ),
        ("row", "col"),
        scatter_dimension=0,
        tiled=True,
    ).astype(jnp.bfloat16)
    act_local = lax.all_gather(act_share, "col", axis=0, tiled=True) * flat_keep
    partial_value = jnp.dot(gradients, basis_out, preferred_element_type=jnp.float32)
    rot_grad = lax.psum(partial_value, "row").astype(jnp.bfloat16)
    height = act_local.shape[0]
    width = rot_grad.shape[1]
    act_blocks = act_local.reshape(height, sequences, -1)
    grad_blocks = rot_grad.reshape(sequences, -1, width)
    products = jnp.einsum(
        "rsl,slc->rsc", act_blocks, grad_blocks, preferred_element_type=jnp.float32
    )
    products = products * scales[None, :, None]
    return jnp.mean(products * products, axis=1)


def in_hbm(value):
    return pltpu.with_memory_space_constraint(value, pltpu.HBM)


def columns_by_rows(weights, rows):
    return lax.dot_general(
        weights, rows, (((0,), (1,)), ((), ())), preferred_element_type=jnp.float32
    )


def pieces(depth):
    return [(at, min(CUT, depth - at)) for at in range(0, depth, CUT)]


def fetch_block(block, gradients, buffer, sems):
    length, depth = buffer.shape
    start = pl.multiple_of(block * length, length)
    return [
        pltpu.make_async_copy(
            gradients.at[pl.ds(start, length), pl.ds(at, size)],
            buffer.at[:, pl.ds(at, size)],
            sems.at[i],
        )
        for i, (at, size) in enumerate(pieces(depth))
    ]


def rotate_block(copies, weights, buffer, out):
    edges = pieces(buffer.shape[1])
    for i, (at, size) in enumerate(edges):
        for copy in copies[i]:
            copy.wait()
        part = columns_by_rows(weights[at : at + size, :], buffer[:, at : at + size])
        if i == 0:
            out[...] = part
        else:
            out[...] += part


def grad_kernel(block, gradients, basis, out, weights, buffer, grad_sems, basis_sems):
    copies = []
    edges = pieces(buffer.shape[1])
    for i, copy in enumerate(fetch_block(block[0], gradients, buffer, grad_sems)):
        at, size = edges[i]
        part = pltpu.make_async_copy(
            basis.at[pl.ds(at, size), :], weights.at[pl.ds(at, size), :], basis_sems.at[i]
        )
        part.start()
        copy.start()
        copies.append((part, copy))
    rotate_block(copies, weights, buffer, out)


def rotate_grad(block, gradients, basis_out, length):
    depth, width = basis_out.shape
    steps = len(pieces(depth))
    return pl.pallas_call(
        grad_kernel,
        in_specs=[SMEM, HBM, HBM],
        out_specs=VMEM,
        out_shape=jax.ShapeDtypeStruct((width, length), jnp.float32),
        scratch_shapes=[
            pltpu.VMEM((depth, width), basis_out.dtype),
            pltpu.VMEM((length, depth), jnp.bfloat16),
            pltpu.SemaphoreType.DMA((steps,)),
            pltpu.SemaphoreType.DMA((steps,)),
        ],
        compiler_params=pltpu.CompilerParams(vmem_limit_bytes=14 * 2**20),
        cost_estimate=pl.CostEstimate(
            flops=2 * length * depth * width,
            bytes_accessed=2 * depth * (length + width),
            transcendentals=0,
        ),
    )(jnp.reshape(block, (1,)), in_hbm(gradients), in_hbm(basis_out))


def act_kernel(where, act, basis, far_act, far_basis, *outs):
    quarter, length = outs[0].shape
    z, core, x = where[0], where[4], where[5]
    span = pl.ds(pl.multiple_of(core * 2 * quarter, 2 * quarter), 2 * quarter)
    near = basis[:, span]
    far = far_basis[:, span]
    for i, step in enumerate((3, 2, 1, 0)):
        rows = pl.ds(pl.multiple_of((z ^ step) * length, length), length)
        product = columns_by_rows(near, act[rows, :]) + columns_by_rows(far, far_act[rows, :])
        low, high = product[:quarter], product[quarter:]
        outs[2 * i][...] = jnp.where(x == 0, low, high)
        outs[2 * i + 1][...] = jnp.where(x == 0, high, low)


def rotate_act(where, activations, basis_in, far_act, far_basis, length):
    shape = jax.ShapeDtypeStruct((basis_in.shape[1] // 4, length), jnp.float32)
    return pl.pallas_call(
        act_kernel,
        in_specs=[SMEM, VMEM, VMEM, VMEM, VMEM],
        out_specs=[VMEM] * 8,
        out_shape=[shape] * 8,
        compiler_params=pltpu.CompilerParams(vmem_limit_bytes=6 * 2**20),
        cost_estimate=pl.CostEstimate(
            flops=2 * activations.size * basis_in.shape[1],
            bytes_accessed=4 * activations.size,
            transcendentals=0,
        ),
    )(where, activations, basis_in, far_act, far_basis)


def tile_kernel(order, ids, act, grad, own, *sends):
    sequences, rows = ids.shape[0], own.shape[0]
    keep = (ids[pl.ds(order[0], 1), :] != 0).astype(jnp.float32)
    weight = 1.0 / jnp.sqrt(jnp.sum(keep, axis=1, keepdims=True))
    keep = keep.astype(jnp.bfloat16)
    for slot, out in enumerate((own, *sends)):
        piece = act[pl.ds(pl.multiple_of(order[slot] * rows, rows), rows), :] * keep
        product = lax.dot_general(
            piece, grad[...], (((1,), (1,)), ((), ())), preferred_element_type=jnp.float32
        )
        product = product * weight
        out[...] = (product * product * (1.0 / sequences)).astype(out.dtype)


def make_tile(order, token_ids, act, grad):
    sequences = token_ids.shape[0]
    rows, width = act.shape[0] // sequences, grad.shape[0]
    return pl.pallas_call(
        tile_kernel,
        in_specs=[SMEM, VMEM, VMEM, VMEM],
        out_specs=[VMEM] * sequences,
        out_shape=[jax.ShapeDtypeStruct((rows, width), jnp.float32)]
        + [jax.ShapeDtypeStruct((rows, width), jnp.bfloat16)] * (sequences - 1),
        compiler_params=pltpu.CompilerParams(vmem_limit_bytes=16 * 2**20),
        cost_estimate=pl.CostEstimate(flops=1, bytes_accessed=1, transcendentals=0),
    )(order, token_ids, act, grad)


def swap(value, axis, step, size=4):
    return lax.ppermute(value, axis, [(i, i ^ step) for i in range(size)])


def pack(value, up):
    return (value * up).astype(jnp.float16)


def unpack(value, up):
    return value.astype(jnp.float32) * (1.0 / up)


def line_shards(activations, basis_in, gradients, basis_out, token_ids):
    length = token_ids.shape[1]
    z = lax.axis_index("row").astype(jnp.int32)
    place = lax.axis_index("col").astype(jnp.int32)
    core, x = place & 1, place >> 1
    quarter = basis_in.shape[1] // 4
    middle = basis_out.shape[1] // 2
    tie = lax.optimization_barrier
    order = jnp.stack([z, z ^ 2, z ^ 3, z ^ 1, core, x])

    far_act, far_basis = swap(activations, "col", 1), swap(basis_in, "col", 1)
    third = rotate_grad(z ^ 3, gradients, basis_out, length)
    third = pack(third, GRAD_UP)
    got_third = swap(third, "row", 1)

    far_act, far_basis, third = tie((far_act, far_basis, third))
    mine_3, other_3, mine_2, other_2, mine_1, other_1, mine_0, other_0 = rotate_act(
        order, activations, basis_in, far_act, far_basis, length
    )
    out_3 = pack(other_3, ACT_UP)
    out_210 = pack(jnp.stack([other_2, other_1, other_0]), ACT_UP)
    got_3 = swap(out_3, "col", 2)
    got_210 = swap(out_210, "col", 2)

    block, out_3, out_210 = tie((z ^ 2, out_3, out_210))
    second = rotate_grad(block, gradients, basis_out, length)
    got_third, second = tie((got_third, second))
    upper_2 = pack(second[:middle] + unpack(got_third[:middle], GRAD_UP), GRAD_UP)
    got_upper_2 = swap(upper_2, "row", 2)
    got_third, second, upper_2 = tie((got_third, second, upper_2))
    got_3, upper_2 = tie((got_3, upper_2))
    act_3 = pack(mine_3 + unpack(got_3, ACT_UP), ACT_UP)
    over_3 = swap(act_3, "row", 1)

    block, act_3, upper_2 = tie((z ^ 1, act_3, upper_2))
    first = rotate_grad(block, gradients, basis_out, length)
    got_210, over_3, first = tie((got_210, over_3, first))
    act_2 = pack(mine_2 + unpack(got_210[0], ACT_UP) + unpack(over_3, ACT_UP), ACT_UP)
    over_2 = swap(act_2, "row", 2)
    act_1 = pack(mine_1 + unpack(got_210[1], ACT_UP), ACT_UP)
    act_0 = mine_0 + unpack(got_210[2], ACT_UP)
    over_1 = swap(act_1, "row", 1)
    first, act_2, act_1, act_0 = tie((first, act_2, act_1, act_0))
    first_out = pack(first, GRAD_UP)
    got_first = swap(first_out, "row", 1)
    got_third, first_out = tie((got_third, first_out))
    lower_2 = pack(second[middle:] + unpack(got_third[middle:], GRAD_UP), GRAD_UP)
    block, first_out, lower_2 = tie((z, first_out, lower_2))
    own = rotate_grad(block, gradients, basis_out, length)
    over_1, over_2, got_upper_2, own = tie((over_1, over_2, got_upper_2, own))
    act = act_0 + unpack(over_1, ACT_UP) + unpack(over_2, ACT_UP)
    act = act.astype(jnp.bfloat16)
    got_lower_2 = swap(lower_2, "row", 2)
    across = swap(act, "col", 2)
    pair = jnp.where(x == 0, jnp.stack([act, across]), jnp.stack([across, act]))
    pair = pair.reshape(2 * quarter, length)
    other = swap(pair, "col", 1)
    whole = jnp.where(core == 0, jnp.stack([pair, other]), jnp.stack([other, pair]))
    whole = whole.reshape(4 * quarter, length)
    got_second = jnp.concatenate([got_upper_2, got_lower_2])
    grad = own + unpack(got_first, GRAD_UP) + unpack(got_second, GRAD_UP)
    tile, to_2, to_3, to_1 = make_tile(order, token_ids, whole, grad.astype(jnp.bfloat16))
    from_2 = swap(to_2, "row", 2)
    from_3 = swap(to_3, "row", 3)
    from_1 = swap(to_1, "row", 1)
    return (
        tile
        + from_2.astype(jnp.float32)
        + from_3.astype(jnp.float32)
        + from_1.astype(jnp.float32)
    )


def solution(mesh):
    in_specs = (
        P("groups", ("row", "col")),
        P(("groups", "row", "col"), None),
        P("groups", "row"),
        P(("groups", "row"), "col"),
        P(),
    )
    out_specs = P(("groups", "row"), "col")
    rows, columns = mesh.shape["row"], mesh.shape["col"]

    def shards(*arrays):
        fits = rows == 4 and columns == 4 and arrays[4].shape[0] == rows
        return (line_shards if fits else plain_shards)(*arrays)

    return jax.shard_map(shards, mesh=mesh, in_specs=in_specs, out_specs=out_specs, check_vma=False)
```
